128 devices in a mesh: dom: 32 (over z, y, core), serve: 4 (over x).
Axes of the slice: x: 4, y: 4, z: 4, core: 2. Of those that a mesh axis runs over, the one named last changes fastest.
Arguments:
- embedding: float32 [262144, 256], P(('dom', 'serve')), may hold values from -40 to 40
- edge_blocks: bfloat16 [2048, 8, 128, 128], P(('dom', 'serve')), may hold values from -0.5 to 0.5
- adjacency: int32 [2048, 8], replicated, may hold values from 0 to 2047, as said below
- degrees: int32 [2048], replicated, may hold values from 2 to 8
- hash_ids: int32 [1024, 1], P('dom'), may hold values from 0 to 3; in each aligned block of 8 rows (0 to 7, 8 to 15, ...) at most 4 rows name the same one
- candidates: int32 [1024, 4], P('dom'), may hold values from 0 to 31
- head_weights: bfloat16 [4, 256, 256], replicated, may hold values from -4 to 4
Outputs:
- refreshed: float32 [262144, 256], P(('dom', 'serve'))
- task_scores: float32 [4, 2048, 128], P(None, ('dom', 'serve'))
The draws below stay inside these ranges and needn't reach their ends.
Inputs may be any that keep to these rules, and one draw needn't show every extreme that they name: `adjacency`: A block's neighbours are item blocks if it is a user block and user blocks if it is an item block; the 8 neighbours of one block lie on 8 different devices; all neighbour slots of one device's blocks name blocks of any one device at most 1 times, and some device exactly 1 times. `hash_ids`: among the 8 user blocks of one device no shard is named more than 4 times, a bound that some block reaches.
All inputs are finite; a program needn't handle non-finite values.
Results may differ from the reference program's by a relative error of at most 0.0022.
Values may be sent and summed in bfloat16 or wider, within the bound.
No kernel may reach another device: no remote copies, remote signals or barrier semaphores. Data moves between devices by JAX's collectives and lax.ppermute only.
A program may use at most 128 MiB of HBM per device.

```python
import math
import jax
import jax.numpy as jnp
import numpy as np
from jax import lax

D = 256
ROWS = 128
K = 8
TASKS = 4
CB = 4
BLK_DEV = 16
UBLK = 8
IBLK = 8
CAPS = 4
NBLK = 2048
NUB = 1024
SLOTS_ALL = 2048
N_DOM = 32
N_SERVE = 4


def draw_adjacency(key, part):
    key = jax.random.fold_in(key, 11)
    device_count = N_DOM * N_SERVE
    slot_count = BLK_DEV * K
    first_key, second_key = jax.random.split(key)
    device_keys = jax.random.split(first_key, device_count)
    orders = jax.vmap(lambda single: jax.random.permutation(single, device_count))(device_keys)
    position = jnp.arange(slot_count, dtype=jnp.int32) % device_count
    owners = orders[:, position]
    half_count = BLK_DEV // 2
    offsets = jax.random.randint(second_key, (device_count, slot_count), 0, half_count)
    local_block = jnp.arange(slot_count, dtype=jnp.int32) // K
    local_ids = jnp.where(local_block[None, :] < half_count, half_count + offsets, offsets)
    return (owners * BLK_DEV + local_ids).reshape(NBLK, K).astype(jnp.int32)


def draw_embedding(key, part):
    key = jax.random.fold_in(key, 23)
    row_key, column_key, common_key, noise_key = jax.random.split(key, 4)
    row_count = NBLK * ROWS
    low_log = math.log(0.3)
    high_log = math.log(3.0)
    row_scale = jnp.exp(jax.random.uniform(row_key, (row_count, 1), jnp.float32, low_log, high_log))
    column_scale = jnp.exp(jax.random.uniform(column_key, (1, D), jnp.float32, low_log, high_log)) / 1.4
    common = jnp.clip(jax.random.normal(common_key, (1, D), jnp.float32), -3.0, 3.0)
    noise = jnp.clip(jax.random.normal(noise_key, (row_count, D), jnp.float32), -4.0, 4.0)
    share = 0.7
    return (row_scale * column_scale * (noise + share * common)).astype(jnp.float32)


def with_ends(entries, key, least, high):
    longest = entries.shape.index(max(entries.shape))
    spots = []
    for shift in (0, 1):
        where = [jax.random.randint(jax.random.fold_in(key, axis), (), 0, length) for axis, length in enumerate(entries.shape)]
        where[longest] = (where[longest] + shift) % entries.shape[longest]
        spots.append(tuple(where))
    return entries.at[spots[0]].set(least).at[spots[1]].set(high)


def level_of(own_key, dims, shards, smallest, high):
    def one(dim, blocks):
        draws = jax.random.uniform(jax.random.fold_in(jax.random.fold_in(own_key, 6), dim), (blocks,), jnp.float32, smallest / len(shards), high / len(shards))
        return jnp.repeat(jnp.exp(draws), dims[dim] // blocks).reshape((-1,) + (1,) * (len(dims) - dim - 1))

    factor_of = one(*shards[0])
    for cut in shards[1:]:
        factor_of = factor_of * one(*cut)
    return factor_of


def assign_block(rng, own, number, rows, amount, top, bound, lean):
    ranking = jax.random.permutation(rng, amount)
    packed, ordinary = load_shares(amount, rows * top, bound, lean, True), load_shares(amount, rows * top, bound, lean, False)
    places = jnp.arange(amount)

    def named(lengths, turn):
        used = int((lengths > 0).sum())
        fixed = max(1, used // 4)
        moved = fixed + (places - fixed + turn * (used - fixed)) % max(1, amount - fixed)
        return jnp.zeros((amount,), jnp.int32).at[ranking[jnp.where(places < fixed, places, moved)]].set(jnp.asarray(lengths, jnp.int32))

    lengths = jnp.where(number % 4 == 0, named(packed, number // 4), named(ordinary, number - number // 4 - 1))
    mixed = jax.random.permutation(jax.random.fold_in(own, 3), amount)
    giver, sink = mixed[0:amount // 2 * 2:2], mixed[1:amount // 2 * 2:2]
    slack = jnp.minimum(lengths[giver] - 1, bound - lengths[sink]) // 2
    slack = jnp.where((giver == ranking[0]) | (sink == ranking[0]) | (lengths[sink] == 0), 0, jnp.maximum(slack, 0))
    moved = jax.random.randint(jax.random.fold_in(own, 4), (amount // 2,), 0, 1 << 20) % (slack + 1)
    lengths = lengths.at[giver].add(-moved).at[sink].add(moved)
    members = jnp.searchsorted(jnp.cumsum(lengths), jnp.arange(rows * top), side="right").astype(jnp.int32)
    table = members.reshape(top, rows).T
    table = table[jax.random.permutation(jax.random.fold_in(own, 1), rows)]
    turn = jax.random.randint(jax.random.fold_in(own, 2), (rows, 1), 0, top)
    return jnp.take_along_axis(table, (jnp.arange(top)[None, :] + turn) % top, axis=1)


def load_shares(amount, total, bound, lean, full):
    portions = [(1 << 20) // math.isqrt(standing ** lean) + 1 for standing in range(1, amount + 1)]
    largest = bound if full else min(bound, max(-(-total // amount), total * portions[0] // sum(portions)))
    least = 1 if total - largest >= amount - 1 else 0
    given, spare = [largest] + [least] * (amount - 1), total - largest - least * (amount - 1)
    while spare > 0:
        free = [i for i in range(1, amount) if given[i] < largest] or [i for i in range(1, amount) if given[i] < bound]
        pool, left = sum([portions[i] for i in free]), spare
        for i in free:
            extra = min(bound - given[i], max(1, left * portions[i] // pool), spare)
            given[i] = given[i] + extra
            spare = spare - extra
    return np.array(given)


def normal_values(key, shape, spread, reach, shards=(), kind=jnp.bfloat16):
    array = jax.random.normal(key, shape, jnp.float32) * spread
    if len(shards) > 0:
        array = level_of(key, shape, shards, -0.22, 0.18) * array
    return jnp.clip(array, min=-reach, max=reach).astype(kind)


def setup_inputs(seed: int = 0) -> dict:
    arg_keys = jax.random.split(jax.random.key(seed), 8)
    embedding = draw_embedding(jax.random.fold_in(arg_keys[7], 71), 0)
    edge_blocks = normal_values(arg_keys[1], (NBLK, K, ROWS, ROWS), ROWS ** -0.5, 0.5, ((0, 128),))
    adjacency = draw_adjacency(jax.random.fold_in(arg_keys[7], 71), 0)
    degrees = with_ends(jax.random.randint(arg_keys[3], (NBLK,), 2, 9), jax.random.fold_in(arg_keys[3], 1), 2, 8).astype(jnp.int32)
    hash_ids_keys = jax.random.split(jax.random.fold_in(arg_keys[4], 1), NUB // UBLK)
    hash_ids_turns = jax.random.permutation(jax.random.fold_in(arg_keys[4], 3), NUB // UBLK)
    hash_ids = jax.vmap(lambda own, number: assign_block(jax.random.fold_in(arg_keys[4], 2), own, number, UBLK, N_SERVE, 1, CAPS, 2))(hash_ids_keys, hash_ids_turns).reshape((NUB, 1))
    candidates = with_ends(jax.random.randint(arg_keys[5], (NUB, CB), 0, N_SERVE * IBLK), jax.random.fold_in(arg_keys[5], 1), 0, (N_SERVE * IBLK) - 1).astype(jnp.int32)
    head_weights = normal_values(arg_keys[6], (TASKS, D, D), 0.75, 4.0)
    return dict(embedding=embedding, edge_blocks=edge_blocks, adjacency=adjacency, degrees=degrees, hash_ids=hash_ids, candidates=candidates, head_weights=head_weights)


def reference(embedding, edge_blocks, adjacency, degrees, hash_ids, candidates, head_weights):
    block_count, neighbours, block_rows, _ = edge_blocks.shape
    feature_width = embedding.shape[1]
    degree_float = degrees.astype(jnp.float32)

    def propagate(layer_input):
        source_blocks = layer_input.astype(jnp.bfloat16).reshape(block_count, block_rows, feature_width)

        def one_block(operands):
            edge_tile, block_ids, own_degree = operands
            fetched = jnp.take(source_blocks, block_ids, axis=0).astype(jnp.float32)
            products = jnp.einsum('kij,kjd->kid', edge_tile.astype(jnp.float32), fetched)
            normalizer = 1.0 / jnp.sqrt(own_degree * jnp.take(degree_float, block_ids, axis=0))
            return lax.optimization_barrier(jnp.sum(products * normalizer[:, None, None], axis=0))
        result = lax.map(one_block, (edge_blocks, adjacency, degree_float))
        return result.reshape(block_count * block_rows, feature_width)
    first = propagate(embedding)
    second = propagate(first)
    refreshed = (embedding + first + second) / 3.0
    final_blocks = refreshed.astype(jnp.bfloat16).reshape(block_count, block_rows, feature_width)
    device_count = N_DOM * N_SERVE
    user_count = hash_ids.shape[0]
    shard_of = hash_ids[:, 0]
    grouped = shard_of.reshape(device_count, UBLK)
    shard_hot = (grouped[:, :, None] == jnp.arange(N_SERVE, dtype=jnp.int32)[None, None, :]).astype(jnp.int32)
    earlier = jnp.cumsum(shard_hot, axis=1) - shard_hot
    user_rank = lax.optimization_barrier(jnp.sum(earlier * shard_hot, axis=2)).reshape(user_count)
    user_ids = jnp.arange(user_count, dtype=jnp.int32)
    device_of = user_ids // UBLK
    dom_of = device_of // N_SERVE
    source_of = device_of % N_SERVE
    slot = ((dom_of * N_SERVE + shard_of) * N_SERVE + source_of) * CAPS + user_rank
    user_block = device_of * BLK_DEV + user_ids % UBLK
    item_block = (dom_of[:, None] * N_SERVE + candidates // IBLK) * BLK_DEV + UBLK + candidates % IBLK
    scale = 1.0 / math.sqrt(feature_width)
    weights_float = head_weights.astype(jnp.float32)

    def head(operands):
        user_index, item_index = operands
        user_rows = jnp.take(final_blocks, user_index, axis=0).astype(jnp.float32)
        projected = jnp.einsum('rd,kde->kre', user_rows, weights_float).astype(jnp.bfloat16)
        projected = lax.optimization_barrier(projected).astype(jnp.float32)
        item_rows = jnp.take(final_blocks, item_index, axis=0).reshape(-1, feature_width).astype(jnp.float32)
        affinity = jnp.einsum('kre,ne->krn', projected, item_rows) * scale
        return lax.optimization_barrier(jnp.mean(jax.nn.sigmoid(affinity), axis=2))
    per_user = lax.map(head, (user_block, item_block))
    task_scores = jnp.zeros((TASKS, SLOTS_ALL, block_rows), jnp.float32)
    task_scores = task_scores.at[:, slot].set(jnp.moveaxis(per_user, 0, 1))
    return (refreshed, task_scores)
```

```python
import functools
import math

import jax
import jax.numpy as jnp
from jax import lax
from jax.experimental import pallas as pl
from jax.experimental.pallas import tpu as pltpu
from jax.sharding import Mesh, PartitionSpec as P

AXES = ("z", "y", "core", "x")
SIZES = (4, 4, 2, 4)
DOM = ("z", "y", "core")
ORDER = ("z", "x", "y", "core")

BLOCKS = 16
HALF = 8
NEAR = 8
ROWS = 128
WIDTH = 256
DEVICES = 128
NBLK = DEVICES * BLOCKS
TASKS = 4
CANDS = 4
SERVE = 4
CAPS = 4
BF16 = jnp.bfloat16
F32 = jnp.float32
ANY = pl.BlockSpec(memory_space=pl.ANY)
SMEM = pl.BlockSpec(memory_space=pltpu.SMEM)
VMEM = pl.BlockSpec(memory_space=pltpu.VMEM)
DMA = pltpu.SemaphoreType.DMA


def params(mib):
    return pltpu.CompilerParams(vmem_limit_bytes=mib * 1024 * 1024)


def cost(flops, mib, transcendentals=0):
    return pl.CostEstimate(
        flops=flops, bytes_accessed=mib * 1024 * 1024, transcendentals=transcendentals
    )


def place_of(device):
    coords, rest = {}, device
    for axis, size in reversed(list(zip(AXES, SIZES))):
        coords[axis] = rest % size
        rest = rest // size
    place = 0
    for axis in ORDER:
        place = place * SIZES[AXES.index(axis)] + coords[axis]
    return place


PLACES = [place_of(device) for device in range(DEVICES)]


def first_kernel(adj_ref, x_ref, out_ref, loc_ref, held, found, found_smem, sem):
    me = lax.axis_index(AXES)
    adj = adj_ref[...]
    hits = jnp.where(adj // BLOCKS == me, adj % BLOCKS, 0)
    for step in (1, 2, 4, 8):
        hits = hits + pltpu.roll(hits, NBLK - step, 1)
    found[...] = jnp.sum(hits, axis=0, keepdims=True)
    copy = pltpu.make_async_copy(found, found_smem, sem)
    copy.start()
    held[...] = x_ref[...].astype(BF16)
    copy.wait()
    for device, place in enumerate(PLACES):
        block = found_smem[0, device * BLOCKS]
        loc_ref[place] = block
        out_ref[place] = held[block]


def first_messages(adjacency, embedding):
    return pl.pallas_call(
        first_kernel,
        in_specs=[VMEM, VMEM],
        out_specs=[VMEM, SMEM],
        out_shape=[
            pltpu.VMEM((DEVICES, ROWS, WIDTH), BF16),
            jax.ShapeDtypeStruct((DEVICES,), jnp.int32),
        ],
        scratch_shapes=[
            pltpu.VMEM((BLOCKS, ROWS, WIDTH), BF16),
            pltpu.VMEM((1, NBLK), jnp.int32),
            pltpu.SMEM((1, NBLK), jnp.int32),
            DMA,
        ],
        compiler_params=params(8),
        cost_estimate=cost(0, 10),
        name="first_messages",
    )(adjacency, embedding)


def load_lists(adj_hbm, lists, sem):
    me = lax.axis_index(AXES)
    window = pl.ds(pl.multiple_of(me // NEAR * ROWS, ROWS), ROWS)
    copy = pltpu.make_async_copy(adj_hbm.at[:, window], lists, sem)
    copy.start()
    copy.wait()
    return me


def gathered_sum(me, g, lists, degree_ref, edge_ref, arrived_ref):
    own = degree_ref[me * BLOCKS + g]
    total = None
    for k in range(NEAR):
        far = lists[k, me % NEAR * BLOCKS + g]
        degree = (own * degree_ref[far]).astype(F32)
        product = jnp.dot(
            edge_ref[g, k], arrived_ref[place_of(far // BLOCKS)], preferred_element_type=F32
        )
        product = product * (1.0 / jnp.sqrt(jnp.full((1, WIDTH), degree)))
        total = product if total is None else total + product
    return total


def layer_one_kernel(
    loc_ref, degree_ref, adj_hbm, edge_ref, arrived_ref, e1_ref, out_ref, held, lists, sem
):
    me = load_lists(adj_hbm, lists, sem)

    def step(g, carry):
        total = gathered_sum(me, g, lists, degree_ref, edge_ref, arrived_ref)
        e1_ref[g] = total
        held[g] = total.astype(BF16)
        return carry

    lax.fori_loop(0, BLOCKS, step, 0)

    def send(q, carry):
        out_ref[q] = held[loc_ref[q]]
        return carry

    lax.fori_loop(0, DEVICES, send, 0, unroll=4)


def layer_one(loc, degrees, adjacency, edge_blocks, arrived):
    return pl.pallas_call(
        layer_one_kernel,
        in_specs=[SMEM, SMEM, ANY, VMEM, VMEM],
        out_specs=[VMEM, VMEM],
        out_shape=[
            pltpu.VMEM((BLOCKS, ROWS, WIDTH), F32),
            pltpu.VMEM((DEVICES, ROWS, WIDTH), BF16),
        ],
        scratch_shapes=[
            pltpu.VMEM((BLOCKS, ROWS, WIDTH), BF16),
            pltpu.SMEM((NEAR, ROWS), jnp.int32),
            DMA,
        ],
        compiler_params=params(8),
        cost_estimate=cost(2 * BLOCKS * NEAR * ROWS * ROWS * WIDTH, 22),
        name="layer_one",
    )(loc, degrees, adjacency, edge_blocks, arrived)


def layer_two_kernel(*refs, base, project):
    degree_ref, adj_hbm, edge_ref, arrived_ref, e0_ref, e1_ref = refs[:6]
    if project:
        weight_ref, _, refreshed_hbm, final_ref = refs[6:10]
    else:
        refreshed_hbm, final_ref = refs[6:8]
    refreshed, lists, sem, out_sem = refs[-4:]
    me = load_lists(adj_hbm, lists, sem)

    def step(i, carry):
        g = base + i
        total = gathered_sum(me, g, lists, degree_ref, edge_ref, arrived_ref)
        value = (e0_ref[g] + e1_ref[g] + total) / 3.0
        refreshed[i] = value
        pltpu.make_async_copy(refreshed.at[i], refreshed_hbm.at[g], out_sem).start()
        rows = value.astype(BF16)
        if project:
            for t in range(TASKS):
                z = jnp.dot(rows, weight_ref[t], preferred_element_type=F32).astype(BF16)
                final_ref[i, t * ROWS : (t + 1) * ROWS] = z * (0.5 / math.sqrt(WIDTH))
        else:
            final_ref[i] = rows
        return carry

    lax.fori_loop(0, HALF, step, 0)
    pltpu.make_async_copy(refreshed, refreshed, out_sem).wait()


def layer_two(
    degrees, adjacency, edge_blocks, arrived, embedding, e1, base, weights=None, refreshed=None
):
    project = weights is not None
    in_specs = [SMEM, ANY, VMEM, VMEM, VMEM, VMEM]
    operands = [degrees, adjacency, edge_blocks, arrived, embedding, e1]
    aliases, rows = {}, ROWS
    if project:
        in_specs += [VMEM, ANY]
        operands += [weights, refreshed]
        aliases, rows = {7: 0}, TASKS * ROWS
    flops = 2 * HALF * ROWS * WIDTH * (NEAR * ROWS + (TASKS * WIDTH if project else 0))
    return pl.pallas_call(
        functools.partial(layer_two_kernel, base=base, project=project),
        in_specs=in_specs,
        out_specs=[ANY, VMEM],
        out_shape=[
            jax.ShapeDtypeStruct((BLOCKS, ROWS, WIDTH), F32),
            pltpu.VMEM((HALF, rows, WIDTH), BF16),
        ],
        scratch_shapes=[
            pltpu.VMEM((HALF, ROWS, WIDTH), F32),
            pltpu.SMEM((NEAR, ROWS), jnp.int32),
            DMA,
            DMA,
        ],
        input_output_aliases=aliases,
        compiler_params=params(8),
        cost_estimate=cost(flops, 10),
        name="layer_two_users" if project else "layer_two_items",
    )(*operands)


def score_kernel(hash_ref, cand_ref, z_ref, *refs):
    pieces, out_ref, items = refs[:-2], refs[-2], refs[-1]
    my_serve = lax.axis_index("x")
    at = 0
    for piece in pieces:
        size = piece.shape[0]
        items[at : at + size] = piece[...]
        at += size
    out_ref[...] = jnp.zeros_like(out_ref)

    def step(g, carry):
        user = my_serve * HALF + g
        shard = hash_ref[0, user]
        rank = jnp.int32(0)
        for other in range(HALF - 1):
            same = (hash_ref[0, my_serve * HALF + other] == shard) & (other < g)
            rank = rank + same.astype(jnp.int32)
        total = jnp.zeros((8, TASKS * ROWS), F32)
        for j in range(CANDS):
            cand = cand_ref[j, user]
            back = (my_serve - cand // HALF + SERVE) % SERVE
            affinity = lax.dot_general(
                items[back * HALF + cand % HALF],
                z_ref[g],
                (((1,), (1,)), ((), ())),
                preferred_element_type=F32,
            )
            curved = jnp.tanh(affinity).reshape(ROWS // 8, 8, TASKS * ROWS)
            total = total + jnp.sum(curved, axis=0)
        mean = 0.5 + (0.5 / (CANDS * ROWS)) * jnp.sum(total, axis=0, keepdims=True)
        for t in range(TASKS):
            out_ref[shard * CAPS + rank, t : t + 1, :] = mean[:, t * ROWS : (t + 1) * ROWS]
        return carry

    lax.fori_loop(0, HALF, step, 0)


def score(hashes, cands, z, pieces):
    count = HALF * TASKS * ROWS * CANDS * ROWS
    return pl.pallas_call(
        score_kernel,
        in_specs=[SMEM, SMEM, VMEM] + [VMEM] * len(pieces),
        out_specs=VMEM,
        out_shape=pltpu.VMEM((SERVE * CAPS, TASKS, ROWS), F32),
        scratch_shapes=[pltpu.VMEM((SERVE * HALF, ROWS, WIDTH), BF16)],
        compiler_params=params(8),
        cost_estimate=cost(2 * count * WIDTH, 5, count),
        name="score",
    )(hashes, cands, z, *pieces)


def exchange(messages):
    return lax.all_to_all(messages, ORDER, split_axis=0, concat_axis=0, tiled=True)


def shift(blocks, by):
    return lax.ppermute(blocks, "x", [(s, (s + by) % SERVE) for s in range(SERVE)])


def on_device(embedding, edge_blocks, adjacency, degrees, hash_ids, candidates, head_weights):
    blocks = embedding.reshape(BLOCKS, ROWS, WIDTH)
    lists = adjacency.T
    messages, loc = first_messages(lists, blocks)
    arrived = exchange(messages)
    e1, messages = layer_one(loc, degrees, lists, edge_blocks, arrived)
    arrived = exchange(messages)
    shared = (degrees, lists, edge_blocks, arrived, blocks, e1)
    refreshed, items = layer_two(*shared, HALF)
    pieces = [
        items,
        shift(items, 1),
        shift(items[: HALF // 2], 2),
        shift(items[HALF // 2 :], 2),
        shift(items, 3),
    ]
    refreshed, z = layer_two(*shared, 0, head_weights, refreshed)
    scores = score(hash_ids.T, candidates.T, z, pieces)
    scores = scores.reshape(SERVE, CAPS, TASKS, ROWS)
    landed = lax.all_to_all(scores, "x", split_axis=0, concat_axis=0, tiled=True)
    task_scores = jnp.moveaxis(landed.reshape(SERVE * CAPS, TASKS, ROWS), 1, 0)
    return refreshed.reshape(BLOCKS * ROWS, WIDTH), task_scores


def solution(mesh):
    fine = Mesh(mesh.devices.reshape(SIZES), AXES)
    placed = (
        P(AXES, None),
        P(AXES, None, None, None),
        P(),
        P(),
        P(DOM, None),
        P(DOM, None),
        P(),
    )
    return jax.shard_map(
        on_device,
        mesh=fine,
        in_specs=placed,
        out_specs=(P(AXES, None), P(None, AXES, None)),
        check_vma=False,
    )
```

```python
import functools
import math

import jax
import jax.numpy as jnp
from jax import lax
from jax.experimental import pallas as pl
from jax.experimental.pallas import tpu as pltpu
from jax.sharding import Mesh, PartitionSpec as P

AXES = ("z", "y", "core", "x")
SIZES = (4, 4, 2, 4)
DOM = ("z", "y", "core")
ORDER = ("z", "x", "y", "core")

BLOCKS = 16
HALF = 8
PIECE = 4
NEAR = 8
ROWS = 128
WIDTH = 256
DEVICES = 128
NBLK = DEVICES * BLOCKS
LANES = 128
LINES = NBLK // LANES
TASKS = 4
CANDS = 4
SERVE = 4
CAPS = 4
BF16 = jnp.bfloat16
F32 = jnp.float32
ANY = pl.BlockSpec(memory_space=pl.ANY)
SMEM = pl.BlockSpec(memory_space=pltpu.SMEM)
VMEM = pl.BlockSpec(memory_space=pltpu.VMEM)
DMA = pltpu.SemaphoreType.DMA


def params(mib):
    return pltpu.CompilerParams(vmem_limit_bytes=mib * 1024 * 1024)


def cost(flops, mib, transcendentals=0):
    return pl.CostEstimate(
        flops=flops, bytes_accessed=mib * 1024 * 1024, transcendentals=transcendentals
    )


def place_of(device):
    coords, rest = {}, device
    for axis, size in reversed(list(zip(AXES, SIZES))):
        coords[axis] = rest % size
        rest = rest // size
    place = 0
    for axis in ORDER:
        place = place * SIZES[AXES.index(axis)] + coords[axis]
    return place


PLACES = [place_of(device) for device in range(DEVICES)]


def first_kernel(
    adj_hbm, degree_hbm, x_hbm, out_ref, plan_ref,
    adj, degrees, x, held, plan, adj_sem, degree_sem, x_sem, plan_sem,
):
    me = lax.axis_index(AXES)
    adj_copy = pltpu.make_async_copy(adj_hbm, adj, adj_sem)
    adj_copy.start()
    degree_copy = pltpu.make_async_copy(degree_hbm, degrees, degree_sem)
    degree_copy.start()
    x_copies = [
        pltpu.make_async_copy(x_hbm.at[pl.ds(i, PIECE)], x.at[pl.ds(i, PIECE)], x_sem.at[i // PIECE])
        for i in range(0, BLOCKS, PIECE)
    ]
    for copy in x_copies:
        copy.start()

    adj_copy.wait()
    listed = adj[...]
    hits = jnp.where(listed // BLOCKS == me, listed % BLOCKS, 0)
    for step in (1, 2, 4, 8):
        hits = hits + pltpu.roll(hits, NBLK - step, 1)
    hits = jnp.sum(hits, axis=0, keepdims=True)
    for i in range(LINES):
        plan_ref[i : i + 1] = hits[:, i * LANES : (i + 1) * LANES]

    degree_copy.wait()
    mine = adj[:, pl.ds(pl.multiple_of(me // NEAR * LANES, LANES), LANES)]
    far = jnp.zeros_like(mine)
    for i in range(LINES):
        line = jnp.broadcast_to(degrees[i : i + 1], mine.shape)
        line = jnp.take_along_axis(line, mine % LANES, axis=1, mode="promise_in_bounds")
        far = jnp.where(mine // LANES == i, line, far)
    own = degrees[pl.ds(me // NEAR, 1)]
    plan_ref[LINES:] = place_of(mine // BLOCKS) + far * own * DEVICES

    plan_copy = pltpu.make_async_copy(plan_ref, plan, plan_sem)
    plan_copy.start()
    for i, copy in enumerate(x_copies):
        copy.wait()
        piece = slice(i * PIECE, (i + 1) * PIECE)
        held[piece] = x[piece].astype(BF16)
    plan_copy.wait()
    send(plan, held, out_ref)


def send(plan, held, out_ref):
    for device, place in enumerate(PLACES):
        at = device * BLOCKS
        out_ref[place] = held[plan[at // LANES, at % LANES]]


def first_messages(adjacency, degrees, embedding):
    return pl.pallas_call(
        first_kernel,
        in_specs=[ANY, ANY, ANY],
        out_specs=[VMEM, VMEM],
        out_shape=[
            pltpu.VMEM((DEVICES, ROWS, WIDTH), BF16),
            pltpu.VMEM((LINES + NEAR, LANES), jnp.int32),
        ],
        scratch_shapes=[
            pltpu.VMEM((NEAR, NBLK), jnp.int32),
            pltpu.VMEM((LINES, LANES), jnp.int32),
            pltpu.VMEM((BLOCKS, ROWS, WIDTH), F32),
            pltpu.VMEM((BLOCKS, ROWS, WIDTH), BF16),
            pltpu.SMEM((LINES + NEAR, LANES), jnp.int32),
            DMA,
            DMA,
            DMA((BLOCKS // PIECE,)),
            DMA,
        ],
        compiler_params=params(8),
        cost_estimate=cost(0, 10),
        name="first_messages",
    )(*[pltpu.with_memory_space_constraint(a, pltpu.HBM) for a in (adjacency, degrees, embedding)])


def gathered_sum(g, plan_ref, edge_ref, arrived_ref):
    column = lax.axis_index(AXES) % NEAR * BLOCKS + g
    total = None
    for k in range(NEAR):
        word = plan_ref[LINES + k, column]
        degree = (word // DEVICES).astype(F32)
        product = jnp.dot(
            edge_ref[g, k], arrived_ref[word % DEVICES], preferred_element_type=F32
        )
        product = product * (1.0 / jnp.sqrt(jnp.full((1, WIDTH), degree)))
        total = product if total is None else total + product
    return total


def layer_one_kernel(plan_ref, edge_ref, arrived_ref, e1_ref, out_ref, held):
    for g in range(BLOCKS):
        total = gathered_sum(g, plan_ref, edge_ref, arrived_ref)
        e1_ref[g] = total
        held[g] = total.astype(BF16)

    send(plan_ref, held, out_ref)


def layer_one(plan, edge_blocks, arrived):
    return pl.pallas_call(
        layer_one_kernel,
        in_specs=[SMEM, VMEM, VMEM],
        out_specs=[VMEM, VMEM],
        out_shape=[
            pltpu.VMEM((BLOCKS, ROWS, WIDTH), F32),
            pltpu.VMEM((DEVICES, ROWS, WIDTH), BF16),
        ],
        scratch_shapes=[pltpu.VMEM((BLOCKS, ROWS, WIDTH), BF16)],
        compiler_params=params(8),
        cost_estimate=cost(2 * BLOCKS * NEAR * ROWS * ROWS * WIDTH, 22),
        name="layer_one",
    )(plan, edge_blocks, arrived)


def items_kernel(plan_ref, edge_ref, arrived_ref, e0_ref, e1_ref, refreshed_ref, *final_refs):
    for i in range(HALF):
        g = HALF + i
        total = gathered_sum(g, plan_ref, edge_ref, arrived_ref)
        value = (e0_ref[g] + e1_ref[g] + total) / 3.0
        refreshed_ref[i] = value
        final_refs[i // PIECE][i % PIECE] = value.astype(BF16)


def layer_two_items(plan, *arrays):
    return pl.pallas_call(
        items_kernel,
        in_specs=[SMEM] + [VMEM] * 4,
        out_specs=[VMEM] * 3,
        out_shape=[pltpu.VMEM((HALF, ROWS, WIDTH), F32)]
        + [pltpu.VMEM((PIECE, ROWS, WIDTH), BF16)] * 2,
        compiler_params=params(8),
        cost_estimate=cost(2 * HALF * ROWS * WIDTH * NEAR * ROWS, 10),
        name="layer_two_items",
    )(plan, *arrays)


def users_kernel(
    plan_ref, edge_ref, arrived_ref, e0_ref, e1_ref, weight_ref, items_ref, out_hbm, z_ref,
    users, user_sem, item_sem,
):
    item_copy = pltpu.make_async_copy(items_ref, out_hbm.at[pl.ds(HALF, HALF)], item_sem)
    item_copy.start()
    for g in range(HALF):
        total = gathered_sum(g, plan_ref, edge_ref, arrived_ref)
        value = (e0_ref[g] + e1_ref[g] + total) / 3.0
        users[g] = value
        rows = value.astype(BF16)
        for t in range(TASKS):
            z = jnp.dot(rows, weight_ref[t], preferred_element_type=F32).astype(BF16)
            z_ref[g, t * ROWS : (t + 1) * ROWS] = z * (0.5 / math.sqrt(WIDTH))
    user_copy = pltpu.make_async_copy(users, out_hbm.at[pl.ds(0, HALF)], user_sem)
    user_copy.start()
    item_copy.wait()
    user_copy.wait()


def layer_two_users(plan, *arrays):
    flops = 2 * HALF * ROWS * WIDTH * (NEAR * ROWS + TASKS * WIDTH)
    return pl.pallas_call(
        users_kernel,
        in_specs=[SMEM] + [VMEM] * 6,
        out_specs=[ANY, VMEM],
        out_shape=[
            jax.ShapeDtypeStruct((BLOCKS, ROWS, WIDTH), F32),
            pltpu.VMEM((HALF, TASKS * ROWS, WIDTH), BF16),
        ],
        scratch_shapes=[pltpu.VMEM((HALF, ROWS, WIDTH), F32), DMA, DMA],
        compiler_params=params(8),
        cost_estimate=cost(flops, 10),
        name="layer_two_users",
    )(plan, *arrays)


def score_kernel(hash_ref, cand_ref, z_ref, *refs):
    pieces, out_ref, items = refs[:-2], refs[-2], refs[-1]
    my_serve = lax.axis_index("x")
    at = 0
    for piece in pieces:
        size = piece.shape[0]
        items[at : at + size] = piece[...]
        at += size
    out_ref[...] = jnp.zeros_like(out_ref)

    def step(g, carry):
        user = my_serve * HALF + g
        shard = hash_ref[0, user]
        rank = jnp.int32(0)
        for other in range(HALF - 1):
            same = (hash_ref[0, my_serve * HALF + other] == shard) & (other < g)
            rank = rank + same.astype(jnp.int32)
        rows = []
        for j in range(CANDS):
            cand = cand_ref[j, user]
            back = (my_serve - cand // HALF + SERVE) % SERVE
            rows.append(items[back * HALF + cand % HALF])
        affinity = lax.dot_general(
            jnp.concatenate(rows, axis=0),
            z_ref[g],
            (((1,), (1,)), ((), ())),
            preferred_element_type=F32,
        )
        total = jnp.sum(jnp.tanh(affinity), axis=0, keepdims=True)
        mean = 0.5 + (0.5 / (CANDS * ROWS)) * total
        for t in range(TASKS):
            out_ref[shard * CAPS + rank, t : t + 1, :] = mean[:, t * ROWS : (t + 1) * ROWS]
        return carry

    lax.fori_loop(0, HALF, step, 0, unroll=2)


def score(hashes, cands, z, pieces):
    count = HALF * TASKS * ROWS * CANDS * ROWS
    return pl.pallas_call(
        score_kernel,
        in_specs=[SMEM, SMEM, VMEM] + [VMEM] * len(pieces),
        out_specs=VMEM,
        out_shape=pltpu.VMEM((SERVE * CAPS, TASKS, ROWS), F32),
        scratch_shapes=[pltpu.VMEM((SERVE * HALF, ROWS, WIDTH), BF16)],
        compiler_params=params(8),
        cost_estimate=cost(2 * count * WIDTH, 5, count),
        name="score",
    )(hashes, cands, z, *pieces)


def exchange(messages):
    return lax.all_to_all(messages, ORDER, split_axis=0, concat_axis=0, tiled=True)


def shift(blocks, by):
    return lax.ppermute(blocks, "x", [(s, (s + by) % SERVE) for s in range(SERVE)])


def on_device(embedding, edge_blocks, adjacency, degrees, hash_ids, candidates, head_weights):
    blocks = embedding.reshape(BLOCKS, ROWS, WIDTH)
    messages, plan = first_messages(adjacency.T, degrees.reshape(LINES, LANES), blocks)
    arrived = exchange(messages)
    e1, messages = layer_one(plan, edge_blocks, arrived)
    arrived = exchange(messages)
    shared = (plan, edge_blocks, arrived, blocks, e1)
    refreshed, items_a, items_b = layer_two_items(*shared)
    left_a, right_b = shift(items_a, 1), shift(items_b, 3)
    left_b, right_a = shift(items_b, 1), shift(items_a, 3)
    refreshed, z = layer_two_users(*shared, head_weights, refreshed)
    left_a, right_b, z = lax.optimization_barrier((left_a, right_b, z))
    far_a, far_b = shift(left_a, 1), shift(right_b, 3)
    pieces = [items_a, items_b, left_a, left_b, far_a, far_b, right_a, right_b]
    scores = score(hash_ids.T, candidates.T, z, pieces)
    scores = scores.reshape(SERVE, CAPS, TASKS, ROWS)
    landed = lax.all_to_all(scores, "x", split_axis=0, concat_axis=0, tiled=True)
    task_scores = jnp.moveaxis(landed.reshape(SERVE * CAPS, TASKS, ROWS), 1, 0)
    return refreshed.reshape(BLOCKS * ROWS, WIDTH), task_scores


def solution(mesh):
    fine = Mesh(mesh.devices.reshape(SIZES), AXES)
    placed = (
        P(AXES, None),
        P(AXES, None, None, None),
        P(),
        P(),
        P(DOM, None),
        P(DOM, None),
        P(),
    )
    return jax.shard_map(
        on_device,
        mesh=fine,
        in_specs=placed,
        out_specs=(P(AXES, None), P(None, AXES, None)),
        check_vma=False,
    )
```

```python
import functools
import math

import jax
import jax.numpy as jnp
from jax import lax
from jax.experimental import pallas as pl
from jax.experimental.pallas import tpu as pltpu
from jax.sharding import Mesh, PartitionSpec as P

AXES = ("z", "y", "core", "x")
SIZES = (4, 4, 2, 4)
DOM = ("z", "y", "core")
ORDER = ("z", "x", "y", "core")

BLOCKS = 16
HALF = 8
PIECE = 4
NEAR = 8
ROWS = 128
WIDTH = 256
DEVICES = 128
NBLK = DEVICES * BLOCKS
LANES = 128
LINES = NBLK // LANES
TASKS = 4
CANDS = 4
SERVE = 4
CAPS = 4
BF16 = jnp.bfloat16
F32 = jnp.float32
ANY = pl.BlockSpec(memory_space=pl.ANY)
SMEM = pl.BlockSpec(memory_space=pltpu.SMEM)
VMEM = pl.BlockSpec(memory_space=pltpu.VMEM)
DMA = pltpu.SemaphoreType.DMA


def params(mib):
    return pltpu.CompilerParams(vmem_limit_bytes=mib * 1024 * 1024)


def cost(flops, mib, transcendentals=0):
    return pl.CostEstimate(
        flops=flops, bytes_accessed=mib * 1024 * 1024, transcendentals=transcendentals
    )


def place_of(device):
    coords, rest = {}, device
    for axis, size in reversed(list(zip(AXES, SIZES))):
        coords[axis] = rest % size
        rest = rest // size
    place = 0
    for axis in ORDER:
        place = place * SIZES[AXES.index(axis)] + coords[axis]
    return place


PLACES = [place_of(device) for device in range(DEVICES)]


def first_kernel(
    adj_hbm, degree_hbm, x_hbm, out_ref, plan_ref,
    adj, degrees, x, held, plan, adj_sem, degree_sem, x_sem, plan_sem,
):
    me = lax.axis_index(AXES)
    adj_copy = pltpu.make_async_copy(adj_hbm, adj, adj_sem)
    adj_copy.start()
    degree_copy = pltpu.make_async_copy(degree_hbm, degrees, degree_sem)
    degree_copy.start()
    x_copies = [
        pltpu.make_async_copy(x_hbm.at[pl.ds(i, PIECE)], x.at[pl.ds(i, PIECE)], x_sem.at[i // PIECE])
        for i in range(0, BLOCKS, PIECE)
    ]
    for copy in x_copies:
        copy.start()

    adj_copy.wait()
    listed = adj[...]
    hits = jnp.where(listed // BLOCKS == me, listed % BLOCKS, 0)
    for step in (1, 2, 4, 8):
        hits = hits + pltpu.roll(hits, NBLK - step, 1)
    hits = jnp.sum(hits, axis=0, keepdims=True)
    for i in range(LINES):
        plan_ref[i : i + 1] = hits[:, i * LANES : (i + 1) * LANES]

    degree_copy.wait()
    mine = adj[:, pl.ds(pl.multiple_of(me // NEAR * LANES, LANES), LANES)]
    far = jnp.zeros_like(mine)
    for i in range(LINES):
        line = jnp.broadcast_to(degrees[i : i + 1], mine.shape)
        line = jnp.take_along_axis(line, mine % LANES, axis=1, mode="promise_in_bounds")
        far = jnp.where(mine // LANES == i, line, far)
    own = degrees[pl.ds(me // NEAR, 1)]
    plan_ref[LINES:] = place_of(mine // BLOCKS) + far * own * DEVICES

    plan_copy = pltpu.make_async_copy(plan_ref, plan, plan_sem)
    plan_copy.start()
    for i, copy in enumerate(x_copies):
        copy.wait()
        piece = slice(i * PIECE, (i + 1) * PIECE)
        held[piece] = x[piece].astype(BF16)
    plan_copy.wait()
    send(plan, held, out_ref)


def send(plan, held, out_ref):
    for device, place in enumerate(PLACES):
        at = device * BLOCKS
        out_ref[place] = held[plan[at // LANES, at % LANES]]


def first_messages(adjacency, degrees, embedding):
    return pl.pallas_call(
        first_kernel,
        in_specs=[ANY, ANY, ANY],
        out_specs=[VMEM, VMEM],
        out_shape=[
            pltpu.VMEM((DEVICES, ROWS, WIDTH), BF16),
            pltpu.VMEM((LINES + NEAR, LANES), jnp.int32),
        ],
        scratch_shapes=[
            pltpu.VMEM((NEAR, NBLK), jnp.int32),
            pltpu.VMEM((LINES, LANES), jnp.int32),
            pltpu.VMEM((BLOCKS, ROWS, WIDTH), F32),
            pltpu.VMEM((BLOCKS, ROWS, WIDTH), BF16),
            pltpu.SMEM((LINES + NEAR, LANES), jnp.int32),
            DMA,
            DMA,
            DMA((BLOCKS // PIECE,)),
            DMA,
        ],
        compiler_params=params(8),
        cost_estimate=cost(0, 10),
        name="first_messages",
    )(*[pltpu.with_memory_space_constraint(a, pltpu.HBM) for a in (adjacency, degrees, embedding)])


def gathered_sum(g, plan_ref, edge_ref, arrived_ref):
    column = lax.axis_index(AXES) % NEAR * BLOCKS + g
    total = None
    for k in range(NEAR):
        word = plan_ref[LINES + k, column]
        degree = (word // DEVICES).astype(F32)
        product = jnp.dot(
            edge_ref[g, k], arrived_ref[word % DEVICES], preferred_element_type=F32
        )
        product = product * (1.0 / jnp.sqrt(jnp.full((1, WIDTH), degree)))
        total = product if total is None else total + product
    return total


def layer_one_kernel(plan_ref, edge_ref, arrived_ref, e1_ref, out_ref, held):
    for g in range(BLOCKS):
        total = gathered_sum(g, plan_ref, edge_ref, arrived_ref)
        e1_ref[g] = total
        held[g] = total.astype(BF16)

    send(plan_ref, held, out_ref)


def layer_one(plan, edge_blocks, arrived):
    return pl.pallas_call(
        layer_one_kernel,
        in_specs=[SMEM, VMEM, VMEM],
        out_specs=[VMEM, VMEM],
        out_shape=[
            pltpu.VMEM((BLOCKS, ROWS, WIDTH), F32),
            pltpu.VMEM((DEVICES, ROWS, WIDTH), BF16),
        ],
        scratch_shapes=[pltpu.VMEM((BLOCKS, ROWS, WIDTH), BF16)],
        compiler_params=params(8),
        cost_estimate=cost(2 * BLOCKS * NEAR * ROWS * ROWS * WIDTH, 22),
        name="layer_one",
    )(plan, edge_blocks, arrived)


def items_kernel(plan_ref, edge_ref, arrived_ref, e0_ref, e1_ref, refreshed_ref, *final_refs):
    for i in range(HALF):
        g = HALF + i
        total = gathered_sum(g, plan_ref, edge_ref, arrived_ref)
        value = (e0_ref[g] + e1_ref[g] + total) / 3.0
        refreshed_ref[i] = value
        final_refs[i // PIECE][i % PIECE] = value.astype(BF16)


def layer_two_items(plan, *arrays):
    return pl.pallas_call(
        items_kernel,
        in_specs=[SMEM] + [VMEM] * 4,
        out_specs=[VMEM] * 3,
        out_shape=[pltpu.VMEM((HALF, ROWS, WIDTH), F32)]
        + [pltpu.VMEM((PIECE, ROWS, WIDTH), BF16)] * 2,
        compiler_params=params(8),
        cost_estimate=cost(2 * HALF * ROWS * WIDTH * NEAR * ROWS, 10),
        name="layer_two_items",
    )(plan, *arrays)


def users_kernel(
    plan_ref, edge_ref, arrived_ref, e0_ref, e1_ref, weight_ref, items_ref, out_hbm, z_ref,
    users, user_sem, item_sem,
):
    item_copy = pltpu.make_async_copy(items_ref, out_hbm.at[pl.ds(HALF, HALF)], item_sem)
    item_copy.start()
    for g in range(HALF):
        total = gathered_sum(g, plan_ref, edge_ref, arrived_ref)
        value = (e0_ref[g] + e1_ref[g] + total) / 3.0
        users[g] = value
        rows = value.astype(BF16)
        for t in range(TASKS):
            z = jnp.dot(rows, weight_ref[t], preferred_element_type=F32).astype(BF16)
            z_ref[g, t * ROWS : (t + 1) * ROWS] = z * (0.5 / math.sqrt(WIDTH))
    user_copy = pltpu.make_async_copy(users, out_hbm.at[pl.ds(0, HALF)], user_sem)
    user_copy.start()
    item_copy.wait()
    user_copy.wait()


def layer_two_users(plan, *arrays):
    flops = 2 * HALF * ROWS * WIDTH * (NEAR * ROWS + TASKS * WIDTH)
    return pl.pallas_call(
        users_kernel,
        in_specs=[SMEM] + [VMEM] * 6,
        out_specs=[ANY, VMEM],
        out_shape=[
            jax.ShapeDtypeStruct((BLOCKS, ROWS, WIDTH), F32),
            pltpu.VMEM((HALF, TASKS * ROWS, WIDTH), BF16),
        ],
        scratch_shapes=[pltpu.VMEM((HALF, ROWS, WIDTH), F32), DMA, DMA],
        compiler_params=params(8),
        cost_estimate=cost(flops, 10),
        name="layer_two_users",
    )(plan, *arrays)


def score_kernel(hash_ref, cand_ref, z_ref, *refs):
    pieces, out_refs, out_ref, items = refs[: -SERVE - 2], refs[-SERVE - 2 : -2], refs[-2], refs[-1]
    my_serve = lax.axis_index("x")
    at = 0
    for piece in pieces:
        size = piece.shape[0]
        items[at : at + size] = piece[...]
        at += size
    out_ref[...] = jnp.zeros_like(out_ref)

    def step(g, carry):
        user = my_serve * HALF + g
        shard = hash_ref[0, user]
        rank = jnp.int32(0)
        for other in range(HALF - 1):
            same = (hash_ref[0, my_serve * HALF + other] == shard) & (other < g)
            rank = rank + same.astype(jnp.int32)
        rows = []
        for j in range(CANDS):
            cand = cand_ref[j, user]
            back = (my_serve - cand // HALF + SERVE) % SERVE
            rows.append(items[back * HALF + cand % HALF])
        affinity = lax.dot_general(
            jnp.concatenate(rows, axis=0),
            z_ref[g],
            (((1,), (1,)), ((), ())),
            preferred_element_type=F32,
        )
        total = jnp.sum(jnp.tanh(affinity), axis=0, keepdims=True)
        mean = 0.5 + (0.5 / (CANDS * ROWS)) * total
        slot = (shard - my_serve + SERVE) % SERVE * CAPS + rank
        for t in range(TASKS):
            out_ref[t, pl.ds(slot, 1), :] = mean[:, t * ROWS : (t + 1) * ROWS]
        return carry

    lax.fori_loop(0, HALF, step, 0, unroll=True)
    for k in range(SERVE):
        out_refs[k][...] = out_ref[:, k * CAPS : (k + 1) * CAPS, :]


def score(hashes, cands, z, pieces):
    count = HALF * TASKS * ROWS * CANDS * ROWS
    return pl.pallas_call(
        score_kernel,
        in_specs=[SMEM, SMEM, VMEM] + [VMEM] * len(pieces),
        out_specs=[VMEM] * SERVE,
        out_shape=[pltpu.VMEM((TASKS, CAPS, ROWS), F32)] * SERVE,
        scratch_shapes=[
            pltpu.VMEM((TASKS, SERVE * CAPS, ROWS), F32),
            pltpu.VMEM((SERVE * HALF, ROWS, WIDTH), BF16),
        ],
        compiler_params=params(8),
        cost_estimate=cost(2 * count * WIDTH, 5, count),
        name="score",
    )(hashes, cands, z, *pieces)


def collect_kernel(*refs):
    parts, out_ref = refs[:-1], refs[-1]
    my_serve = lax.axis_index("x")
    values = [part[...] for part in parts]
    for s in range(SERVE):
        mine = values[0]
        for k in range(1, SERVE):
            mine = jnp.where((my_serve - s + SERVE) % SERVE == k, values[k], mine)
        out_ref[:, s * CAPS : (s + 1) * CAPS, :] = mine


def collect(parts):
    return pl.pallas_call(
        collect_kernel,
        in_specs=[VMEM] * SERVE,
        out_specs=VMEM,
        out_shape=jax.ShapeDtypeStruct((TASKS, SERVE * CAPS, ROWS), F32),
        compiler_params=params(8),
        name="collect",
    )(*parts)


def exchange(messages):
    return lax.all_to_all(messages, ORDER, split_axis=0, concat_axis=0, tiled=True)


def shift(blocks, by):
    return lax.ppermute(blocks, "x", [(s, (s + by) % SERVE) for s in range(SERVE)])


def on_device(embedding, edge_blocks, adjacency, degrees, hash_ids, candidates, head_weights):
    blocks = embedding.reshape(BLOCKS, ROWS, WIDTH)
    messages, plan = first_messages(adjacency.T, degrees.reshape(LINES, LANES), blocks)
    arrived = exchange(messages)
    e1, messages = layer_one(plan, edge_blocks, arrived)
    arrived = exchange(messages)
    shared = (plan, edge_blocks, arrived, blocks, e1)
    refreshed, items_a, items_b = layer_two_items(*shared)
    left_a, right_b = shift(items_a, 1), shift(items_b, 3)
    left_b, right_a = shift(items_b, 1), shift(items_a, 3)
    refreshed, z = layer_two_users(*shared, head_weights, refreshed)
    left_a, right_b, z = lax.optimization_barrier((left_a, right_b, z))
    far_a, far_b = shift(left_a, 1), shift(right_b, 3)
    pieces = [items_a, items_b, left_a, left_b, far_a, far_b, right_a, right_b]
    parts = score(hash_ids.T, candidates.T, z, pieces)
    task_scores = collect([parts[0]] + [shift(parts[k], k) for k in range(1, SERVE)])
    return refreshed.reshape(BLOCKS * ROWS, WIDTH), task_scores


def solution(mesh):
    fine = Mesh(mesh.devices.reshape(SIZES), AXES)
    placed = (
        P(AXES, None),
        P(AXES, None, None, None),
        P(),
        P(),
        P(DOM, None),
        P(DOM, None),
        P(),
    )
    return jax.shard_map(
        on_device,
        mesh=fine,
        in_specs=placed,
        out_specs=(P(AXES, None), P(None, AXES, None)),
        check_vma=False,
    )
```

```python
import functools
import math

import jax
import jax.numpy as jnp
from jax import lax
from jax.experimental import pallas as pl
from jax.experimental.pallas import tpu as pltpu
from jax.sharding import Mesh, PartitionSpec as P

AXES = ("z", "y", "core", "x")
SIZES = (4, 4, 2, 4)
DOM = ("z", "y", "core")
ORDER = ("z", "x", "y", "core")

BLOCKS = 16
HALF = 8
PIECE = 4
NEAR = 8
ROWS = 128
WIDTH = 256
DEVICES = 128
NBLK = DEVICES * BLOCKS
LANES = 128
SHIFT = 7
BITS = 4
LINES = NBLK // LANES
TASKS = 4
CANDS = 4
SERVE = 4
CAPS = 4
BF16 = jnp.bfloat16
F32 = jnp.float32
ANY = pl.BlockSpec(memory_space=pl.ANY)
SMEM = pl.BlockSpec(memory_space=pltpu.SMEM)
VMEM = pl.BlockSpec(memory_space=pltpu.VMEM)
DMA = pltpu.SemaphoreType.DMA


def params(mib):
    return pltpu.CompilerParams(vmem_limit_bytes=mib * 1024 * 1024)


def cost(flops, mib, transcendentals=0):
    return pl.CostEstimate(
        flops=flops, bytes_accessed=mib * 1024 * 1024, transcendentals=transcendentals
    )


def place_of(device):
    coords, rest = {}, device
    for axis, size in reversed(list(zip(AXES, SIZES))):
        coords[axis] = rest % size
        rest = rest // size
    place = 0
    for axis in ORDER:
        place = place * SIZES[AXES.index(axis)] + coords[axis]
    return place


PLACES = [place_of(device) for device in range(DEVICES)]


def first_kernel(
    adj_hbm, degree_hbm, x_hbm, out_ref, plan_ref,
    adj, degrees, x, held, plan, adj_sem, degree_sem, x_sem, plan_sem,
):
    me = lax.axis_index(AXES)
    adj_copy = pltpu.make_async_copy(adj_hbm, adj, adj_sem)
    adj_copy.start()
    degree_copy = pltpu.make_async_copy(degree_hbm, degrees, degree_sem)
    degree_copy.start()
    x_copies = [
        pltpu.make_async_copy(x_hbm.at[pl.ds(i, PIECE)], x.at[pl.ds(i, PIECE)], x_sem.at[i // PIECE])
        for i in range(0, BLOCKS, PIECE)
    ]
    for copy in x_copies:
        copy.start()

    adj_copy.wait()
    listed = adj[...]
    hits = jnp.where(lax.shift_right_logical(listed, BITS) == me, listed & (BLOCKS - 1), 0)
    for step in (1, 2, 4, 8):
        hits = hits + pltpu.roll(hits, NBLK - step, 1)
    hits = jnp.sum(hits, axis=0, keepdims=True)
    for i in range(LINES):
        plan_ref[i : i + 1] = hits[:, i * LANES : (i + 1) * LANES]
    plan_copy = pltpu.make_async_copy(plan_ref.at[pl.ds(0, LINES)], plan, plan_sem)
    plan_copy.start()

    degree_copy.wait()
    mine = adj[:, pl.ds(pl.multiple_of(me // NEAR * LANES, LANES), LANES)]
    far = jnp.zeros_like(mine)
    for i in range(LINES):
        line = jnp.broadcast_to(degrees[i : i + 1], mine.shape)
        line = jnp.take_along_axis(line, mine % LANES, axis=1, mode="promise_in_bounds")
        far = jnp.where(mine // LANES == i, line, far)
    own = degrees[pl.ds(me // NEAR, 1)]
    plan_ref[LINES:] = place_of(mine // BLOCKS) + far * own * DEVICES

    for i, copy in enumerate(x_copies):
        copy.wait()
        piece = slice(i * PIECE, (i + 1) * PIECE)
        held[piece] = x[piece].astype(BF16)
    plan_copy.wait()
    send(plan, held, out_ref)


def send(plan, held, out_ref):
    for device, place in enumerate(PLACES):
        at = device * BLOCKS
        out_ref[place] = held[plan[at // LANES, at % LANES]]


def first_messages(adjacency, degrees, embedding):
    return pl.pallas_call(
        first_kernel,
        in_specs=[ANY, ANY, ANY],
        out_specs=[VMEM, VMEM],
        out_shape=[
            pltpu.VMEM((DEVICES, ROWS, WIDTH), BF16),
            pltpu.VMEM((LINES + NEAR, LANES), jnp.int32),
        ],
        scratch_shapes=[
            pltpu.VMEM((NEAR, NBLK), jnp.int32),
            pltpu.VMEM((LINES, LANES), jnp.int32),
            pltpu.VMEM((BLOCKS, ROWS, WIDTH), F32),
            pltpu.VMEM((BLOCKS, ROWS, WIDTH), BF16),
            pltpu.SMEM((LINES, LANES), jnp.int32),
            DMA,
            DMA,
            DMA((BLOCKS // PIECE,)),
            DMA,
        ],
        compiler_params=params(8),
        cost_estimate=cost(0, 10),
        name="first_messages",
    )(*[pltpu.with_memory_space_constraint(a, pltpu.HBM) for a in (adjacency, degrees, embedding)])


def gathered_sums(blocks, plan_ref, edge_ref, arrived_ref):
    first = (lax.axis_index(AXES) & (NEAR - 1)) * BLOCKS

    def read(g):
        words = [plan_ref[LINES + k, first + g] for k in range(NEAR)]
        places = [word & (DEVICES - 1) for word in words]
        return places, [lax.shift_right_logical(word, SHIFT).astype(F32) for word in words]

    ahead = read(blocks[0])
    for g, later in zip(blocks, list(blocks[1:]) + [None]):
        places, degrees = ahead
        if later is not None:
            ahead = read(later)
        total = None
        for k in range(NEAR):
            norm = 1.0 / jnp.sqrt(jnp.full((1, LANES), degrees[k]))
            product = jnp.dot(edge_ref[g, k], arrived_ref[places[k]], preferred_element_type=F32)
            product = product * jnp.concatenate([norm] * (WIDTH // LANES), axis=1)
            total = product if total is None else total + product
        yield g, total


def layer_one_kernel(plan_ref, edge_ref, arrived_ref, e1_ref, out_ref, held):
    for g, total in gathered_sums(range(BLOCKS), plan_ref, edge_ref, arrived_ref):
        e1_ref[g] = total
        held[g] = total.astype(BF16)

    send(plan_ref, held, out_ref)


def layer_one(plan, edge_blocks, arrived):
    return pl.pallas_call(
        layer_one_kernel,
        in_specs=[SMEM, VMEM, VMEM],
        out_specs=[VMEM, VMEM],
        out_shape=[
            pltpu.VMEM((BLOCKS, ROWS, WIDTH), F32),
            pltpu.VMEM((DEVICES, ROWS, WIDTH), BF16),
        ],
        scratch_shapes=[pltpu.VMEM((BLOCKS, ROWS, WIDTH), BF16)],
        compiler_params=params(8),
        cost_estimate=cost(2 * BLOCKS * NEAR * ROWS * ROWS * WIDTH, 22),
        name="layer_one",
    )(plan, edge_blocks, arrived)


def items_kernel(plan_ref, edge_ref, arrived_ref, e0_ref, e1_ref, refreshed_ref, *final_refs):
    for g, total in gathered_sums(range(HALF, BLOCKS), plan_ref, edge_ref, arrived_ref):
        i = g - HALF
        value = (e0_ref[g] + e1_ref[g] + total) * (1.0 / 3.0)
        refreshed_ref[i] = value
        final_refs[i // PIECE][i % PIECE] = value.astype(BF16)


def layer_two_items(plan, *arrays):
    return pl.pallas_call(
        items_kernel,
        in_specs=[SMEM] + [VMEM] * 4,
        out_specs=[VMEM] * 3,
        out_shape=[pltpu.VMEM((HALF, ROWS, WIDTH), F32)]
        + [pltpu.VMEM((PIECE, ROWS, WIDTH), BF16)] * 2,
        compiler_params=params(8),
        cost_estimate=cost(2 * HALF * ROWS * WIDTH * NEAR * ROWS, 10),
        name="layer_two_items",
    )(plan, *arrays)


def users_kernel(
    plan_ref, edge_ref, arrived_ref, e0_ref, e1_ref, weight_ref, items_ref, out_hbm, z_ref,
    users, user_sem, item_sem,
):
    item_copy = pltpu.make_async_copy(items_ref, out_hbm.at[pl.ds(HALF, HALF)], item_sem)
    item_copy.start()
    for g, total in gathered_sums(range(HALF), plan_ref, edge_ref, arrived_ref):
        value = (e0_ref[g] + e1_ref[g] + total) * (1.0 / 3.0)
        users[g] = value
        rows = value.astype(BF16)
        for t in range(TASKS):
            z = jnp.dot(rows, weight_ref[t], preferred_element_type=F32).astype(BF16)
            z_ref[g, t * ROWS : (t + 1) * ROWS] = z * (0.5 / math.sqrt(WIDTH))
    user_copy = pltpu.make_async_copy(users, out_hbm.at[pl.ds(0, HALF)], user_sem)
    user_copy.start()
    item_copy.wait()
    user_copy.wait()


def layer_two_users(plan, *arrays):
    flops = 2 * HALF * ROWS * WIDTH * (NEAR * ROWS + TASKS * WIDTH)
    return pl.pallas_call(
        users_kernel,
        in_specs=[SMEM] + [VMEM] * 6,
        out_specs=[ANY, VMEM],
        out_shape=[
            jax.ShapeDtypeStruct((BLOCKS, ROWS, WIDTH), F32),
            pltpu.VMEM((HALF, TASKS * ROWS, WIDTH), BF16),
        ],
        scratch_shapes=[pltpu.VMEM((HALF, ROWS, WIDTH), F32), DMA, DMA],
        compiler_params=params(8),
        cost_estimate=cost(flops, 10),
        name="layer_two_users",
    )(plan, *arrays)


def score_kernel(hash_ref, cand_ref, z_ref, *refs):
    pieces, out_refs, out_ref, items = refs[: -SERVE - 2], refs[-SERVE - 2 : -2], refs[-2], refs[-1]
    my_serve = lax.axis_index("x")
    at = 0
    for piece in pieces:
        size = piece.shape[0]
        items[at : at + size] = piece[...]
        at += size
    out_ref[...] = jnp.zeros_like(out_ref)

    def step(g, carry):
        user = my_serve * HALF + g
        shard = hash_ref[0, user]
        rank = jnp.int32(0)
        for other in range(HALF - 1):
            same = (hash_ref[0, my_serve * HALF + other] == shard) & (other < g)
            rank = rank + same.astype(jnp.int32)
        rows = []
        for j in range(CANDS):
            cand = cand_ref[j, user]
            back = (my_serve - cand // HALF + SERVE) % SERVE
            rows.append(items[back * HALF + cand % HALF])
        affinity = lax.dot_general(
            jnp.concatenate(rows, axis=0),
            z_ref[g],
            (((1,), (1,)), ((), ())),
            preferred_element_type=F32,
        )
        total = jnp.sum(jnp.tanh(affinity), axis=0, keepdims=True)
        mean = 0.5 + (0.5 / (CANDS * ROWS)) * total
        slot = (shard - my_serve + SERVE) % SERVE * CAPS + rank
        for t in range(TASKS):
            out_ref[t, pl.ds(slot, 1), :] = mean[:, t * ROWS : (t + 1) * ROWS]
        return carry

    lax.fori_loop(0, HALF, step, 0, unroll=True)
    for k in range(SERVE):
        out_refs[k][...] = out_ref[:, k * CAPS : (k + 1) * CAPS, :]


def score(hashes, cands, z, pieces):
    count = HALF * TASKS * ROWS * CANDS * ROWS
    return pl.pallas_call(
        score_kernel,
        in_specs=[SMEM, SMEM, VMEM] + [VMEM] * len(pieces),
        out_specs=[VMEM] * SERVE,
        out_shape=[pltpu.VMEM((TASKS, CAPS, ROWS), F32)] * SERVE,
        scratch_shapes=[
            pltpu.VMEM((TASKS, SERVE * CAPS, ROWS), F32),
            pltpu.VMEM((SERVE * HALF, ROWS, WIDTH), BF16),
        ],
        compiler_params=params(8),
        cost_estimate=cost(2 * count * WIDTH, 5, count),
        name="score",
    )(hashes, cands, z, *pieces)


def collect_kernel(*refs):
    parts, out_ref = refs[:-1], refs[-1]
    my_serve = lax.axis_index("x")
    values = [part[...] for part in parts]
    for s in range(SERVE):
        mine = values[0]
        for k in range(1, SERVE):
            mine = jnp.where((my_serve - s + SERVE) % SERVE == k, values[k], mine)
        out_ref[:, s * CAPS : (s + 1) * CAPS, :] = mine


def collect(parts):
    return pl.pallas_call(
        collect_kernel,
        in_specs=[VMEM] * SERVE,
        out_specs=VMEM,
        out_shape=jax.ShapeDtypeStruct((TASKS, SERVE * CAPS, ROWS), F32),
        compiler_params=params(8),
        name="collect",
    )(*parts)


def exchange(messages):
    return lax.all_to_all(messages, ORDER, split_axis=0, concat_axis=0, tiled=True)


def shift(blocks, by):
    return lax.ppermute(blocks, "x", [(s, (s + by) % SERVE) for s in range(SERVE)])


def on_device(embedding, edge_blocks, adjacency, degrees, hash_ids, candidates, head_weights):
    blocks = embedding.reshape(BLOCKS, ROWS, WIDTH)
    messages, plan = first_messages(adjacency.T, degrees.reshape(LINES, LANES), blocks)
    arrived = exchange(messages)
    e1, messages = layer_one(plan, edge_blocks, arrived)
    arrived = exchange(messages)
    shared = (plan, edge_blocks, arrived, blocks, e1)
    refreshed, items_a, items_b = layer_two_items(*shared)
    left_a, right_b = shift(items_a, 1), shift(items_b, 3)
    left_b, right_a = shift(items_b, 1), shift(items_a, 3)
    refreshed, z = layer_two_users(*shared, head_weights, refreshed)
    left_a, right_b, z = lax.optimization_barrier((left_a, right_b, z))
    far_a, far_b = shift(left_a, 1), shift(right_b, 3)
    pieces = [items_a, items_b, left_a, left_b, far_a, far_b, right_a, right_b]
    parts = score(hash_ids.T, candidates.T, z, pieces)
    task_scores = collect([parts[0]] + [shift(parts[k], k) for k in range(1, SERVE)])
    return refreshed.reshape(BLOCKS * ROWS, WIDTH), task_scores


def solution(mesh):
    fine = Mesh(mesh.devices.reshape(SIZES), AXES)
    placed = (
        P(AXES, None),
        P(AXES, None, None, None),
        P(),
        P(),
        P(DOM, None),
        P(DOM, None),
        P(),
    )
    return jax.shard_map(
        on_device,
        mesh=fine,
        in_specs=placed,
        out_specs=(P(AXES, None), P(None, AXES, None)),
        check_vma=False,
    )
```

```python
import functools
import math

import jax
import jax.numpy as jnp
from jax import lax
from jax.experimental import pallas as pl
from jax.experimental.pallas import tpu as pltpu
from jax.sharding import Mesh, PartitionSpec as P

AXES = ("z", "y", "core", "x")
SIZES = (4, 4, 2, 4)
DOM = ("z", "y", "core")
ORDER = ("z", "core", "x", "y")

BLOCKS = 16
HALF = 8
PIECE = 4
NEAR = 8
ROWS = 128
WIDTH = 256
DEVICES = 128
NBLK = DEVICES * BLOCKS
LANES = 128
SHIFT = 7
BITS = 4
LINES = NBLK // LANES
TASKS = 4
CANDS = 4
SERVE = 4
CAPS = 4
BF16 = jnp.bfloat16
F32 = jnp.float32
ANY = pl.BlockSpec(memory_space=pl.ANY)
SMEM = pl.BlockSpec(memory_space=pltpu.SMEM)
VMEM = pl.BlockSpec(memory_space=pltpu.VMEM)
DMA = pltpu.SemaphoreType.DMA


def params(mib):
    return pltpu.CompilerParams(vmem_limit_bytes=mib * 1024 * 1024)


def cost(flops, mib, transcendentals=0):
    return pl.CostEstimate(
        flops=flops, bytes_accessed=mib * 1024 * 1024, transcendentals=transcendentals
    )


def place_of(device):
    coords, rest = {}, device
    for axis, size in reversed(list(zip(AXES, SIZES))):
        coords[axis] = rest % size
        rest = rest // size
    place = 0
    for axis in ORDER:
        place = place * SIZES[AXES.index(axis)] + coords[axis]
    return place


PLACES = [place_of(device) for device in range(DEVICES)]


def first_kernel(
    adj_hbm, degree_hbm, x_hbm, out_ref, plan_ref,
    adj, degrees, x, held, plan, adj_sem, degree_sem, x_sem, plan_sem,
):
    me = lax.axis_index(AXES)
    adj_copy = pltpu.make_async_copy(adj_hbm, adj, adj_sem)
    adj_copy.start()
    degree_copy = pltpu.make_async_copy(degree_hbm, degrees, degree_sem)
    degree_copy.start()
    x_copies = [
        pltpu.make_async_copy(x_hbm.at[pl.ds(i, PIECE)], x.at[pl.ds(i, PIECE)], x_sem.at[i // PIECE])
        for i in range(0, BLOCKS, PIECE)
    ]
    for copy in x_copies:
        copy.start()

    adj_copy.wait()
    listed = adj[...]
    hits = jnp.where(lax.shift_right_logical(listed, BITS) == me, listed & (BLOCKS - 1), 0)
    for step in (1, 2, 4, 8):
        hits = hits + pltpu.roll(hits, NBLK - step, 1)
    hits = jnp.sum(hits, axis=0, keepdims=True)
    for i in range(LINES):
        plan_ref[i : i + 1] = hits[:, i * LANES : (i + 1) * LANES]
    plan_copy = pltpu.make_async_copy(plan_ref.at[pl.ds(0, LINES)], plan, plan_sem)
    plan_copy.start()

    degree_copy.wait()
    mine = adj[:, pl.ds(pl.multiple_of(me // NEAR * LANES, LANES), LANES)]
    far = jnp.zeros_like(mine)
    for i in range(LINES):
        line = jnp.broadcast_to(degrees[i : i + 1], mine.shape)
        line = jnp.take_along_axis(line, mine % LANES, axis=1, mode="promise_in_bounds")
        far = jnp.where(mine // LANES == i, line, far)
    own = degrees[pl.ds(me // NEAR, 1)]
    plan_ref[LINES:] = place_of(mine // BLOCKS) + far * own * DEVICES

    for i, copy in enumerate(x_copies):
        copy.wait()
        piece = slice(i * PIECE, (i + 1) * PIECE)
        held[piece] = x[piece].astype(BF16)
    plan_copy.wait()
    send(plan, held, out_ref)


def send(plan, held, out_ref):
    for device, place in enumerate(PLACES):
        at = device * BLOCKS
        out_ref[place] = held[plan[at // LANES, at % LANES]]


def first_messages(adjacency, degrees, embedding):
    return pl.pallas_call(
        first_kernel,
        in_specs=[ANY, ANY, ANY],
        out_specs=[VMEM, VMEM],
        out_shape=[
            pltpu.VMEM((DEVICES, ROWS, WIDTH), BF16),
            pltpu.VMEM((LINES + NEAR, LANES), jnp.int32),
        ],
        scratch_shapes=[
            pltpu.VMEM((NEAR, NBLK), jnp.int32),
            pltpu.VMEM((LINES, LANES), jnp.int32),
            pltpu.VMEM((BLOCKS, ROWS, WIDTH), F32),
            pltpu.VMEM((BLOCKS, ROWS, WIDTH), BF16),
            pltpu.SMEM((LINES, LANES), jnp.int32),
            DMA,
            DMA,
            DMA((BLOCKS // PIECE,)),
            DMA,
        ],
        compiler_params=params(8),
        cost_estimate=cost(0, 10),
        name="first_messages",
    )(*[pltpu.with_memory_space_constraint(a, pltpu.HBM) for a in (adjacency, degrees, embedding)])


def gathered_sums(blocks, plan_ref, edge_ref, arrived_ref):
    first = (lax.axis_index(AXES) & (NEAR - 1)) * BLOCKS

    def read(g):
        words = [plan_ref[LINES + k, first + g] for k in range(NEAR)]
        places = [word & (DEVICES - 1) for word in words]
        return places, [lax.shift_right_logical(word, SHIFT).astype(F32) for word in words]

    ahead = read(blocks[0])
    for g, later in zip(blocks, list(blocks[1:]) + [None]):
        places, degrees = ahead
        if later is not None:
            ahead = read(later)
        total = None
        for k in range(NEAR):
            norm = 1.0 / jnp.sqrt(jnp.full((1, LANES), degrees[k]))
            product = jnp.dot(edge_ref[g, k], arrived_ref[places[k]], preferred_element_type=F32)
            product = product * jnp.concatenate([norm] * (WIDTH // LANES), axis=1)
            total = product if total is None else total + product
        yield g, total


def layer_one_kernel(plan_ref, edge_ref, arrived_ref, e1_ref, out_ref, held):
    for g, total in gathered_sums(range(BLOCKS), plan_ref, edge_ref, arrived_ref):
        e1_ref[g] = total
        held[g] = total.astype(BF16)

    send(plan_ref, held, out_ref)


def layer_one(plan, edge_blocks, arrived):
    return pl.pallas_call(
        layer_one_kernel,
        in_specs=[SMEM, VMEM, VMEM],
        out_specs=[VMEM, VMEM],
        out_shape=[
            pltpu.VMEM((BLOCKS, ROWS, WIDTH), F32),
            pltpu.VMEM((DEVICES, ROWS, WIDTH), BF16),
        ],
        scratch_shapes=[pltpu.VMEM((BLOCKS, ROWS, WIDTH), BF16)],
        compiler_params=params(8),
        cost_estimate=cost(2 * BLOCKS * NEAR * ROWS * ROWS * WIDTH, 22),
        name="layer_one",
    )(plan, edge_blocks, arrived)


def items_kernel(plan_ref, edge_ref, arrived_ref, e0_ref, e1_ref, refreshed_ref, *final_refs):
    for g, total in gathered_sums(range(HALF, BLOCKS), plan_ref, edge_ref, arrived_ref):
        i = g - HALF
        value = (e0_ref[g] + e1_ref[g] + total) * (1.0 / 3.0)
        refreshed_ref[i] = value
        final_refs[i // PIECE][i % PIECE] = value.astype(BF16)


def layer_two_items(plan, *arrays):
    return pl.pallas_call(
        items_kernel,
        in_specs=[SMEM] + [VMEM] * 4,
        out_specs=[VMEM] * 3,
        out_shape=[pltpu.VMEM((HALF, ROWS, WIDTH), F32)]
        + [pltpu.VMEM((PIECE, ROWS, WIDTH), BF16)] * 2,
        compiler_params=params(8),
        cost_estimate=cost(2 * HALF * ROWS * WIDTH * NEAR * ROWS, 10),
        name="layer_two_items",
    )(plan, *arrays)


def users_kernel(
    plan_ref, edge_ref, arrived_ref, e0_ref, e1_ref, weight_ref, items_ref, out_hbm, z_ref,
    users, user_sem, item_sem,
):
    item_copy = pltpu.make_async_copy(items_ref, out_hbm.at[pl.ds(HALF, HALF)], item_sem)
    item_copy.start()
    for g, total in gathered_sums(range(HALF), plan_ref, edge_ref, arrived_ref):
        value = (e0_ref[g] + e1_ref[g] + total) * (1.0 / 3.0)
        users[g] = value
        rows = value.astype(BF16)
        for t in range(TASKS):
            z = jnp.dot(rows, weight_ref[t], preferred_element_type=F32).astype(BF16)
            z_ref[g, t * ROWS : (t + 1) * ROWS] = z * (0.5 / math.sqrt(WIDTH))
    user_copy = pltpu.make_async_copy(users, out_hbm.at[pl.ds(0, HALF)], user_sem)
    user_copy.start()
    item_copy.wait()
    user_copy.wait()


def layer_two_users(plan, *arrays):
    flops = 2 * HALF * ROWS * WIDTH * (NEAR * ROWS + TASKS * WIDTH)
    return pl.pallas_call(
        users_kernel,
        in_specs=[SMEM] + [VMEM] * 6,
        out_specs=[ANY, VMEM],
        out_shape=[
            jax.ShapeDtypeStruct((BLOCKS, ROWS, WIDTH), F32),
            pltpu.VMEM((HALF, TASKS * ROWS, WIDTH), BF16),
        ],
        scratch_shapes=[pltpu.VMEM((HALF, ROWS, WIDTH), F32), DMA, DMA],
        compiler_params=params(8),
        cost_estimate=cost(flops, 10),
        name="layer_two_users",
    )(plan, *arrays)


def score_kernel(hash_ref, cand_ref, z_ref, *refs):
    pieces, out_refs, out_ref, items = refs[: -SERVE - 2], refs[-SERVE - 2 : -2], refs[-2], refs[-1]
    my_serve = lax.axis_index("x")
    at = 0
    for piece in pieces:
        size = piece.shape[0]
        items[at : at + size] = piece[...]
        at += size
    out_ref[...] = jnp.zeros_like(out_ref)

    def step(g, carry):
        user = my_serve * HALF + g
        shard = hash_ref[0, user]
        rank = jnp.int32(0)
        for other in range(HALF - 1):
            same = (hash_ref[0, my_serve * HALF + other] == shard) & (other < g)
            rank = rank + same.astype(jnp.int32)
        rows = []
        for j in range(CANDS):
            cand = cand_ref[j, user]
            back = (my_serve - cand // HALF + SERVE) % SERVE
            rows.append(items[back * HALF + cand % HALF])
        affinity = lax.dot_general(
            jnp.concatenate(rows, axis=0),
            z_ref[g],
            (((1,), (1,)), ((), ())),
            preferred_element_type=F32,
        )
        total = jnp.sum(jnp.tanh(affinity), axis=0, keepdims=True)
        mean = 0.5 + (0.5 / (CANDS * ROWS)) * total
        slot = (shard - my_serve + SERVE) % SERVE * CAPS + rank
        for t in range(TASKS):
            out_ref[t, pl.ds(slot, 1), :] = mean[:, t * ROWS : (t + 1) * ROWS]
        return carry

    lax.fori_loop(0, HALF, step, 0, unroll=True)
    for k in range(SERVE):
        out_refs[k][...] = out_ref[:, k * CAPS : (k + 1) * CAPS, :]


def score(hashes, cands, z, pieces):
    count = HALF * TASKS * ROWS * CANDS * ROWS
    return pl.pallas_call(
        score_kernel,
        in_specs=[SMEM, SMEM, VMEM] + [VMEM] * len(pieces),
        out_specs=[VMEM] * SERVE,
        out_shape=[pltpu.VMEM((TASKS, CAPS, ROWS), F32)] * SERVE,
        scratch_shapes=[
            pltpu.VMEM((TASKS, SERVE * CAPS, ROWS), F32),
            pltpu.VMEM((SERVE * HALF, ROWS, WIDTH), BF16),
        ],
        compiler_params=params(8),
        cost_estimate=cost(2 * count * WIDTH, 5, count),
        name="score",
    )(hashes, cands, z, *pieces)


def collect_kernel(*refs):
    parts, out_ref = refs[:-1], refs[-1]
    my_serve = lax.axis_index("x")
    values = [part[...] for part in parts]
    for s in range(SERVE):
        mine = values[0]
        for k in range(1, SERVE):
            mine = jnp.where((my_serve - s + SERVE) % SERVE == k, values[k], mine)
        out_ref[:, s * CAPS : (s + 1) * CAPS, :] = mine


def collect(parts):
    return pl.pallas_call(
        collect_kernel,
        in_specs=[VMEM] * SERVE,
        out_specs=VMEM,
        out_shape=jax.ShapeDtypeStruct((TASKS, SERVE * CAPS, ROWS), F32),
        compiler_params=params(8),
        name="collect",
    )(*parts)


def exchange(messages):
    return lax.all_to_all(messages, ORDER, split_axis=0, concat_axis=0, tiled=True)


def shift(blocks, by):
    return lax.ppermute(blocks, "x", [(s, (s + by) % SERVE) for s in range(SERVE)])


def on_device(embedding, edge_blocks, adjacency, degrees, hash_ids, candidates, head_weights):
    blocks = embedding.reshape(BLOCKS, ROWS, WIDTH)
    messages, plan = first_messages(adjacency.T, degrees.reshape(LINES, LANES), blocks)
    arrived = exchange(messages)
    e1, messages = layer_one(plan, edge_blocks, arrived)
    arrived = exchange(messages)
    shared = (plan, edge_blocks, arrived, blocks, e1)
    refreshed, items_a, items_b = layer_two_items(*shared)
    left_a, right_b = shift(items_a, 1), shift(items_b, 3)
    left_b, right_a = shift(items_b, 1), shift(items_a, 3)
    refreshed, z = layer_two_users(*shared, head_weights, refreshed)
    left_a, right_b, z = lax.optimization_barrier((left_a, right_b, z))
    far_a, far_b = shift(left_a, 1), shift(right_b, 3)
    pieces = [items_a, items_b, left_a, left_b, far_a, far_b, right_a, right_b]
    parts = score(hash_ids.T, candidates.T, z, pieces)
    task_scores = collect([parts[0]] + [shift(parts[k], k) for k in range(1, SERVE)])
    return refreshed.reshape(BLOCKS * ROWS, WIDTH), task_scores


def solution(mesh):
    fine = Mesh(mesh.devices.reshape(SIZES), AXES)
    placed = (
        P(AXES, None),
        P(AXES, None, None, None),
        P(),
        P(),
        P(DOM, None),
        P(DOM, None),
        P(),
    )
    return jax.shard_map(
        on_device,
        mesh=fine,
        in_specs=placed,
        out_specs=(P(AXES, None), P(None, AXES, None)),
        check_vma=False,
    )
```

```python
import functools
import math

import jax
import jax.numpy as jnp
from jax import lax
from jax.experimental import pallas as pl
from jax.experimental.pallas import tpu as pltpu
from jax.sharding import Mesh, PartitionSpec as P

AXES = ("z", "y", "core", "x")
SIZES = (4, 4, 2, 4)
DOM = ("z", "y", "core")
ORDER = ("z", "core", "x", "y")

BLOCKS = 16
HALF = 8
PIECE = 4
NEAR = 8
ROWS = 128
WIDTH = 256
DEVICES = 128
NBLK = DEVICES * BLOCKS
LANES = 128
SHIFT = 7
BITS = 4
LINES = NBLK // LANES
TASKS = 4
CANDS = 4
SERVE = 4
CAPS = 4
BF16 = jnp.bfloat16
F32 = jnp.float32
ANY = pl.BlockSpec(memory_space=pl.ANY)
SMEM = pl.BlockSpec(memory_space=pltpu.SMEM)
VMEM = pl.BlockSpec(memory_space=pltpu.VMEM)
DMA = pltpu.SemaphoreType.DMA


def params(mib):
    return pltpu.CompilerParams(vmem_limit_bytes=mib * 1024 * 1024)


def cost(flops, mib, transcendentals=0):
    return pl.CostEstimate(
        flops=flops, bytes_accessed=mib * 1024 * 1024, transcendentals=transcendentals
    )


def place_of(device):
    coords, rest = {}, device
    for axis, size in reversed(list(zip(AXES, SIZES))):
        coords[axis] = rest % size
        rest = rest // size
    place = 0
    for axis in ORDER:
        place = place * SIZES[AXES.index(axis)] + coords[axis]
    return place


PLACES = [place_of(device) for device in range(DEVICES)]


def first_kernel(
    adj_hbm, degree_hbm, x_hbm, out_ref, plan_ref,
    adj, degrees, x, held, plan, adj_sem, degree_sem, x_sem, plan_sem,
):
    me = lax.axis_index(AXES)
    adj_copy = pltpu.make_async_copy(adj_hbm, adj, adj_sem)
    adj_copy.start()
    degree_copy = pltpu.make_async_copy(degree_hbm, degrees, degree_sem)
    degree_copy.start()
    x_copies = [
        pltpu.make_async_copy(x_hbm.at[pl.ds(i, PIECE)], x.at[pl.ds(i, PIECE)], x_sem.at[i // PIECE])
        for i in range(0, BLOCKS, PIECE)
    ]
    for copy in x_copies:
        copy.start()

    adj_copy.wait()
    listed = adj[...]
    hits = jnp.where(lax.shift_right_logical(listed, BITS) == me, listed & (BLOCKS - 1), 0)
    for step in (1, 2, 4, 8):
        hits = hits + pltpu.roll(hits, NBLK - step, 1)
    hits = jnp.sum(hits, axis=0, keepdims=True)
    for i in range(LINES):
        plan_ref[i : i + 1] = hits[:, i * LANES : (i + 1) * LANES]
    plan_copy = pltpu.make_async_copy(plan_ref.at[pl.ds(0, LINES)], plan, plan_sem)
    plan_copy.start()

    degree_copy.wait()
    mine = adj[:, pl.ds(pl.multiple_of(me // NEAR * LANES, LANES), LANES)]
    far = jnp.zeros_like(mine)
    for i in range(LINES):
        line = jnp.broadcast_to(degrees[i : i + 1], mine.shape)
        line = jnp.take_along_axis(line, mine % LANES, axis=1, mode="promise_in_bounds")
        far = jnp.where(mine // LANES == i, line, far)
    own = degrees[pl.ds(me // NEAR, 1)]
    plan_ref[LINES:] = place_of(mine // BLOCKS) + far * own * DEVICES

    for i, copy in enumerate(x_copies):
        copy.wait()
        piece = slice(i * PIECE, (i + 1) * PIECE)
        held[piece] = x[piece].astype(BF16)
    plan_copy.wait()
    send(plan, held, out_ref)


def send(plan, held, out_ref):
    for device, place in enumerate(PLACES):
        at = device * BLOCKS
        out_ref[place] = held[plan[at // LANES, at % LANES]]


def first_messages(adjacency, degrees, embedding):
    return pl.pallas_call(
        first_kernel,
        in_specs=[ANY, ANY, ANY],
        out_specs=[VMEM, VMEM],
        out_shape=[
            pltpu.VMEM((DEVICES, ROWS, WIDTH), BF16),
            pltpu.VMEM((LINES + NEAR, LANES), jnp.int32),
        ],
        scratch_shapes=[
            pltpu.VMEM((NEAR, NBLK), jnp.int32),
            pltpu.VMEM((LINES, LANES), jnp.int32),
            pltpu.VMEM((BLOCKS, ROWS, WIDTH), F32),
            pltpu.VMEM((BLOCKS, ROWS, WIDTH), BF16),
            pltpu.SMEM((LINES, LANES), jnp.int32),
            DMA,
            DMA,
            DMA((BLOCKS // PIECE,)),
            DMA,
        ],
        compiler_params=params(8),
        cost_estimate=cost(0, 10),
        name="first_messages",
    )(*[pltpu.with_memory_space_constraint(a, pltpu.HBM) for a in (adjacency, degrees, embedding)])


def gathered_sums(blocks, plan_ref, edge_ref, arrived_ref):
    first = (lax.axis_index(AXES) & (NEAR - 1)) * BLOCKS

    def read(g):
        words = [plan_ref[LINES + k, first + g] for k in range(NEAR)]
        places = [word & (DEVICES - 1) for word in words]
        return places, [lax.shift_right_logical(word, SHIFT).astype(F32) for word in words]

    ahead = read(blocks[0])
    for g, later in zip(blocks, list(blocks[1:]) + [None]):
        places, degrees = ahead
        if later is not None:
            ahead = read(later)
        total = None
        for k in range(NEAR):
            norm = 1.0 / jnp.sqrt(jnp.full((1, LANES), degrees[k]))
            product = jnp.dot(edge_ref[g, k], arrived_ref[places[k]], preferred_element_type=F32)
            product = product * jnp.concatenate([norm] * (WIDTH // LANES), axis=1)
            total = product if total is None else total + product
        yield g, total


def layer_one_kernel(plan_ref, edge_ref, arrived_ref, e1_ref, out_ref, held):
    for g, total in gathered_sums(range(BLOCKS), plan_ref, edge_ref, arrived_ref):
        e1_ref[g] = total
        held[g] = total.astype(BF16)

    send(plan_ref, held, out_ref)


def layer_one(plan, edge_blocks, arrived):
    return pl.pallas_call(
        layer_one_kernel,
        in_specs=[SMEM, VMEM, VMEM],
        out_specs=[VMEM, VMEM],
        out_shape=[
            pltpu.VMEM((BLOCKS, ROWS, WIDTH), F32),
            pltpu.VMEM((DEVICES, ROWS, WIDTH), BF16),
        ],
        scratch_shapes=[pltpu.VMEM((BLOCKS, ROWS, WIDTH), BF16)],
        compiler_params=params(8),
        cost_estimate=cost(2 * BLOCKS * NEAR * ROWS * ROWS * WIDTH, 22),
        name="layer_one",
    )(plan, edge_blocks, arrived)


def items_kernel(plan_ref, edge_ref, arrived_ref, e0_ref, e1_ref, refreshed_ref, *final_refs):
    for g, total in gathered_sums(range(HALF, BLOCKS), plan_ref, edge_ref, arrived_ref):
        i = g - HALF
        value = (e0_ref[g] + e1_ref[g] + total) * (1.0 / 3.0)
        refreshed_ref[i] = value
        final_refs[i // PIECE][i % PIECE] = value.astype(BF16)


def layer_two_items(plan, *arrays):
    return pl.pallas_call(
        items_kernel,
        in_specs=[SMEM] + [VMEM] * 4,
        out_specs=[VMEM] * 3,
        out_shape=[pltpu.VMEM((HALF, ROWS, WIDTH), F32)]
        + [pltpu.VMEM((PIECE, ROWS, WIDTH), BF16)] * 2,
        compiler_params=params(8),
        cost_estimate=cost(2 * HALF * ROWS * WIDTH * NEAR * ROWS, 10),
        name="layer_two_items",
    )(plan, *arrays)


def users_kernel(
    plan_ref, edge_ref, arrived_ref, e0_ref, e1_ref, weight_ref, items_ref, out_hbm, z_ref,
    users, user_sem, item_sem,
):
    item_copy = pltpu.make_async_copy(items_ref, out_hbm.at[pl.ds(HALF, HALF)], item_sem)
    item_copy.start()
    for g, total in gathered_sums(range(HALF), plan_ref, edge_ref, arrived_ref):
        value = (e0_ref[g] + e1_ref[g] + total) * (1.0 / 3.0)
        users[g] = value
        rows = value.astype(BF16)
        for t in range(TASKS):
            z = jnp.dot(rows, weight_ref[t], preferred_element_type=F32).astype(BF16)
            z_ref[g, t * ROWS : (t + 1) * ROWS] = z * (0.5 / math.sqrt(WIDTH))
    user_copy = pltpu.make_async_copy(users, out_hbm.at[pl.ds(0, HALF)], user_sem)
    user_copy.start()
    item_copy.wait()
    user_copy.wait()


def layer_two_users(plan, *arrays):
    flops = 2 * HALF * ROWS * WIDTH * (NEAR * ROWS + TASKS * WIDTH)
    return pl.pallas_call(
        users_kernel,
        in_specs=[SMEM] + [VMEM] * 6,
        out_specs=[ANY, VMEM],
        out_shape=[
            jax.ShapeDtypeStruct((BLOCKS, ROWS, WIDTH), F32),
            pltpu.VMEM((HALF, TASKS * ROWS, WIDTH), BF16),
        ],
        scratch_shapes=[pltpu.VMEM((HALF, ROWS, WIDTH), F32), DMA, DMA],
        compiler_params=params(8),
        cost_estimate=cost(flops, 10),
        name="layer_two_users",
    )(plan, *arrays)


def score_kernel(hash_ref, cand_ref, z_ref, *refs):
    pieces, out_refs, out_ref, items = refs[: -SERVE - 2], refs[-SERVE - 2 : -2], refs[-2], refs[-1]
    my_serve = lax.axis_index("x")
    at = 0
    for piece in pieces:
        size = piece.shape[0]
        items[at : at + size] = piece[...]
        at += size
    out_ref[...] = jnp.zeros_like(out_ref)

    def step(g, carry):
        user = my_serve * HALF + g
        shard = hash_ref[0, user]
        rank = jnp.int32(0)
        for other in range(HALF - 1):
            same = (hash_ref[0, my_serve * HALF + other] == shard) & (other < g)
            rank = rank + same.astype(jnp.int32)
        rows = []
        for j in range(CANDS):
            cand = cand_ref[j, user]
            back = (my_serve - cand // HALF + SERVE) % SERVE
            rows.append(items[back * HALF + cand % HALF])
        affinity = lax.dot_general(
            jnp.concatenate(rows, axis=0),
            z_ref[g],
            (((1,), (1,)), ((), ())),
            preferred_element_type=F32,
        )
        total = jnp.sum(jnp.tanh(affinity), axis=0, keepdims=True)
        mean = 0.5 + (0.5 / (CANDS * ROWS)) * total
        slot = (shard - my_serve + SERVE) % SERVE * CAPS + rank
        for t in range(TASKS):
            out_ref[t, pl.ds(slot, 1), :] = mean[:, t * ROWS : (t + 1) * ROWS]
        return carry

    lax.fori_loop(0, HALF, step, 0, unroll=True)
    for k in range(SERVE):
        out_refs[k][...] = out_ref[:, k * CAPS : (k + 1) * CAPS, :]


def score(hashes, cands, z, pieces):
    count = HALF * TASKS * ROWS * CANDS * ROWS
    return pl.pallas_call(
        score_kernel,
        in_specs=[SMEM, SMEM, VMEM] + [VMEM] * len(pieces),
        out_specs=[VMEM] * SERVE,
        out_shape=[pltpu.VMEM((TASKS, CAPS, ROWS), F32)] * SERVE,
        scratch_shapes=[
            pltpu.VMEM((TASKS, SERVE * CAPS, ROWS), F32),
            pltpu.VMEM((SERVE * HALF, ROWS, WIDTH), BF16),
        ],
        compiler_params=params(8),
        cost_estimate=cost(2 * count * WIDTH, 5, count),
        name="score",
    )(hashes, cands, z, *pieces)


def collect_kernel(*refs):
    parts, out_ref = refs[:-1], refs[-1]
    my_serve = lax.axis_index("x")
    values = [part[...] for part in parts]
    for s in range(SERVE):
        mine = values[0]
        for k in range(1, SERVE):
            mine = jnp.where((my_serve - s + SERVE) % SERVE == k, values[k], mine)
        out_ref[:, s * CAPS : (s + 1) * CAPS, :] = mine


def collect(parts):
    return pl.pallas_call(
        collect_kernel,
        in_specs=[VMEM] * SERVE,
        out_specs=VMEM,
        out_shape=jax.ShapeDtypeStruct((TASKS, SERVE * CAPS, ROWS), F32),
        compiler_params=params(8),
        name="collect",
    )(*parts)


def exchange(messages):
    return lax.all_to_all(messages, ORDER, split_axis=0, concat_axis=0, tiled=True)


def shift(blocks, by):
    return lax.ppermute(blocks, "x", [(s, (s + by) % SERVE) for s in range(SERVE)])


def on_device(embedding, edge_blocks, adjacency, degrees, hash_ids, candidates, head_weights):
    blocks = embedding.reshape(BLOCKS, ROWS, WIDTH)
    messages, plan = first_messages(adjacency.T, degrees.reshape(LINES, LANES), blocks)
    arrived = exchange(messages)
    e1, messages = layer_one(plan, edge_blocks, arrived)
    arrived = exchange(messages)
    shared = (plan, edge_blocks, arrived, blocks, e1)
    refreshed, items_a, items_b = layer_two_items(*shared)
    left_a, right_b = shift(items_a, 1), shift(items_b, 3)
    left_b, right_a = shift(items_b, 1), shift(items_a, 3)
    refreshed, z = layer_two_users(*shared, head_weights, refreshed)
    far_a, far_b = shift(left_a, 1), shift(right_b, 3)
    pieces = [items_a, items_b, left_a, left_b, far_a, far_b, right_a, right_b]
    parts = score(hash_ids.T, candidates.T, z, pieces)
    task_scores = collect([parts[0]] + [shift(parts[k], k) for k in range(1, SERVE)])
    return refreshed.reshape(BLOCKS * ROWS, WIDTH), task_scores


def solution(mesh):
    fine = Mesh(mesh.devices.reshape(SIZES), AXES)
    placed = (
        P(AXES, None),
        P(AXES, None, None, None),
        P(),
        P(),
        P(DOM, None),
        P(DOM, None),
        P(),
    )
    return jax.shard_map(
        on_device,
        mesh=fine,
        in_specs=placed,
        out_specs=(P(AXES, None), P(None, AXES, None)),
        check_vma=False,
    )
```
